32 devices in a mesh: dp: 8 (over z, x), row: 2 (over core), col: 2 (over y).
Axes of the slice: x: 2, y: 2, z: 4, core: 2. Of those that a mesh axis runs over, the one named last changes fastest.
Arguments:
- tokens: bfloat16 [16384, 768], P(('dp', 'row'), 'col'), may hold values from -6 to 6
- segments: int32 [16384], P('dp'), may hold values from 0 to 7, as said below
- positions: int32 [16384], P('dp'), may hold values from 0 to 2047, as said below
- w_qkv: bfloat16 [768, 2304], P('col', 'row'), may hold values from -0.21875 to 0.21875
- b_qkv: float32 [2304], P('row'), may hold values from -4 to 4
- w_dense: bfloat16 [768, 768], P('row', 'col'), may hold values from -1.25 to 1.25
- b_dense: float32 [768], P('col'), may hold values from -4 to 4
- w_in: bfloat16 [768, 3072], P('col', 'row'), may hold values from -0.21875 to 0.21875
- b_in: float32 [3072], P('row'), may hold values from -4 to 4
- w_out: bfloat16 [3072, 768], P('row', 'col'), may hold values from -0.109375 to 0.109375
- b_out: float32 [768], P('col'), may hold values from -4 to 4
- gain_one: float32 [768], P('col'), may hold values from 0.5 to 1.5
- shift_one: float32 [768], P('col'), may hold values from -4 to 4
- gain_two: float32 [768], P('col'), may hold values from 0.5 to 1.5
- shift_two: float32 [768], P('col'), may hold values from -4 to 4
- cotangent: bfloat16 [16384, 768], P(('dp', 'row'), 'col'), may hold values from -6 to 6
Outputs:
- mixed: float32 [16384, 768], P(('dp', 'row'), 'col')
- d_tokens: float32 [16384, 768], P(('dp', 'row'), 'col')
- d_w_qkv: float32 [768, 2304], P('col', 'row')
- d_b_qkv: float32 [2304], P('row')
- d_w_dense: float32 [768, 768], P('row', 'col')
- d_b_dense: float32 [768], P('col')
- d_w_in: float32 [768, 3072], P('col', 'row')
- d_b_in: float32 [3072], P('row')
- d_w_out: float32 [3072, 768], P('row', 'col')
- d_b_out: float32 [768], P('col')
- d_gain_one: float32 [768], P('col')
- d_shift_one: float32 [768], P('col')
- d_gain_two: float32 [768], P('col')
- d_shift_two: float32 [768], P('col')
The draws below stay inside these ranges and needn't reach their ends.
Inputs may be any that keep to these rules, and one draw needn't show every extreme that they name: `segments`: within each pack of 2048 tokens, document numbers start at 0, never fall, and rise by one at each of exactly 7 places, so each pack holds 8 documents. The document that holds position 1024 of a pack begins 2048/16 or more positions before it and ends 2048/16 or more positions after it. Within a document, positions rise by one from token to token; every document of a pack but its first starts at 0; the first ends at position 2047.
All inputs are finite; a program needn't handle non-finite values.
Results may differ from the reference program's by a relative error of at most 0.0094.
Values may be sent and summed in bfloat16 or wider, within the bound.
A program may use at most 192 MiB of HBM per device.

```python
import jax
import jax.numpy as jnp
from jax import lax

D = 768
HEADS = 12
HEAD_DIM = 64
ROT = 16
FF = 3072
SEQ_LEN = 2048
QKV = 2304
TOKENS = 16384


def pack_layout(key):
    pack_count = TOKENS // SEQ_LEN
    places = jnp.arange(SEQ_LEN, dtype=jnp.int32)[None, :]
    middle = SEQ_LEN // 2
    margin_size = jax.random.randint(jax.random.fold_in(key, 2), (pack_count, 1), SEQ_LEN // 16, SEQ_LEN // 4 + 1)
    inside = (places > middle - margin_size) & (places <= middle + margin_size)
    usable = (places > 0) & jnp.logical_not(inside)
    raw_scores = jax.random.randint(jax.random.fold_in(key, 1), (pack_count, SEQ_LEN), 0, SEQ_LEN)
    scores = jnp.where(usable, raw_scores * SEQ_LEN + places, -1).astype(jnp.int32)
    top_scores = lax.top_k(scores, 7)[0]
    chosen = (top_scores % SEQ_LEN).astype(jnp.int32)
    starts = jnp.sum((places[:, :, None] == chosen[:, None, :]).astype(jnp.int32), axis=2).astype(jnp.int32)
    segment_ids = jnp.cumsum(starts, axis=1).astype(jnp.int32)
    opened = jnp.where((starts > 0) | (places == 0), places, 0).astype(jnp.int32)
    doc_begin = lax.cummax(opened, axis=1)
    first_start = jnp.min(chosen, axis=1, keepdims=True)
    position_ids = (places - doc_begin + jnp.where(segment_ids == 0, SEQ_LEN - first_start, 0)).astype(jnp.int32)
    return (segment_ids.reshape(-1), position_ids.reshape(-1))


def draw_segments(key, part):
    segment_ids, position_ids = pack_layout(key)
    return segment_ids


def draw_positions(key, part):
    segment_ids, position_ids = pack_layout(key)
    return position_ids


def block_scale(own_key, dims, cuts, least, top_value):
    def one(dim, parts):
        heights = jax.random.uniform(jax.random.fold_in(jax.random.fold_in(own_key, 6), dim), (parts,), jnp.float32, least / len(cuts), top_value / len(cuts))
        return jnp.repeat(jnp.exp(heights), dims[dim] // parts).reshape((-1,) + (1,) * (len(dims) - dim - 1))

    level = one(*cuts[0])
    for cut in cuts[1:]:
        level = level * one(*cut)
    return level


def normal_values(key, extent, width, most, cuts=(), kind=jnp.bfloat16):
    entries = width * jax.random.normal(key, extent, jnp.float32)
    if cuts:
        entries = entries * block_scale(key, extent, cuts, -0.22, 0.18)
    return jnp.clip(entries, -most, most).astype(kind)


def setup_inputs(seed: int = 0) -> dict:
    keys = jax.random.split(jax.random.key(seed), 17)
    return {
        "tokens": normal_values(keys[0], (TOKENS, D), 1.0, 6.0, ((0, 16), (1, 2))),
        "segments": draw_segments(jax.random.fold_in(keys[16], 71), 0),
        "positions": draw_positions(jax.random.fold_in(keys[16], 71), 0),
        "w_qkv": normal_values(keys[3], (D, QKV), D ** -0.5, 0.21875, ((0, 2), (1, 2))),
        "b_qkv": normal_values(keys[4], (QKV,), 0.3, 4.0, ((0, 2),), jnp.float32),
        "w_dense": normal_values(keys[5], (D, D), (D // 32) ** -0.5, 1.25, ((0, 2), (1, 2))),
        "b_dense": normal_values(keys[6], (D,), 0.3, 4.0, ((0, 2),), jnp.float32),
        "w_in": normal_values(keys[7], (D, FF), D ** -0.5, 0.21875, ((0, 2), (1, 2))),
        "b_in": normal_values(keys[8], (FF,), 0.3, 4.0, ((0, 2),), jnp.float32),
        "w_out": normal_values(keys[9], (FF, D), FF ** -0.5, 0.109375, ((0, 2), (1, 2))),
        "b_out": normal_values(keys[10], (D,), 0.3, 4.0, ((0, 2),), jnp.float32),
        "gain_one": jnp.clip(1.0 + 0.1 * jax.random.normal(keys[11], (D,), jnp.float32), 0.5, 1.5),
        "shift_one": normal_values(keys[12], (D,), 0.3, 4.0, ((0, 2),), jnp.float32),
        "gain_two": jnp.clip(1.0 + 0.1 * jax.random.normal(keys[13], (D,), jnp.float32), 0.5, 1.5),
        "shift_two": normal_values(keys[14], (D,), 0.3, 4.0, ((0, 2),), jnp.float32),
        "cotangent": normal_values(keys[15], (TOKENS, D), 1.0, 6.0, ((0, 16), (1, 2))),
    }


@jax.custom_vjp
def low(v):
    return lax.optimization_barrier(v.astype(jnp.bfloat16)).astype(jnp.float32)

@jax.custom_vjp
def low_back(v):
    return v

def low_keep(v):
    return (low(v), None)

def low_pass(kept, grad):
    return (grad,)

def back_keep(v):
    return (v, None)

def back_low(kept, grad):
    return (low(grad),)
low.defvjp(low_keep, low_pass)
low_back.defvjp(back_keep, back_low)
norm_epsilon = 1e-05
masked_fill = -1e+30

def product(left, right):
    return jnp.dot(left, right, precision=lax.Precision.HIGHEST)

def rotary_tables(position):
    steps = jnp.arange(ROT // 2, dtype=jnp.int32).astype(jnp.float32)
    inverse = 10000.0 ** (-2.0 * steps / ROT)
    angle = position.astype(jnp.float32)[:, None] * inverse[None, :]
    angle = jnp.concatenate([angle, angle], axis=1)
    return (jnp.cos(angle), jnp.sin(angle))

def rotary(part, cosines, sines):
    turned = part[..., :ROT]
    swapped = jnp.concatenate([-turned[..., ROT // 2:], turned[..., :ROT // 2]], axis=-1)
    rotated = turned * cosines[:, None, :] + swapped * sines[:, None, :]
    return jnp.concatenate([rotated, part[..., ROT:]], axis=-1)

def pack_layer(weights, inputs, segment_row, position_row):
    w_qkv, b_qkv, w_dense, b_dense, w_in, b_in, w_out, b_out, gain_one, shift_one, gain_two, shift_two = weights
    length = inputs.shape[0]
    average = lax.optimization_barrier(jnp.mean(inputs, axis=1, keepdims=True))
    centred = inputs - average
    spread = lax.optimization_barrier(jnp.mean(centred * centred, axis=1, keepdims=True))
    normed = centred * lax.rsqrt(spread + norm_epsilon)
    first_in = low(normed * gain_one + shift_one)
    second_in = low(normed * gain_two + shift_two)
    joined_qkv = low_back(product(first_in, w_qkv) + b_qkv).reshape(length, HEADS, 3, HEAD_DIM)
    cosines, sines = rotary_tables(position_row)
    queries = low(rotary(joined_qkv[:, :, 0], cosines, sines))
    keys_rot = low(rotary(joined_qkv[:, :, 1], cosines, sines))
    values_in = low(joined_qkv[:, :, 2])
    scores = low_back(jnp.einsum('qhd,khd->hqk', queries, keys_rot, precision=lax.Precision.HIGHEST) * HEAD_DIM ** (-0.5))
    places = jnp.arange(length, dtype=jnp.int32)
    allowed = (segment_row[:, None] == segment_row[None, :]) & (places[:, None] >= places[None, :])
    masked = jnp.where(allowed[None], scores, masked_fill)
    highest = lax.optimization_barrier(jnp.max(masked, axis=2, keepdims=True))
    lifted = jnp.exp(masked - highest)
    weights_soft = lifted / lax.optimization_barrier(jnp.sum(lifted, axis=2, keepdims=True))
    context = jnp.einsum('hqk,khd->qhd', low(weights_soft), values_in, precision=lax.Precision.HIGHEST)
    context = low_back(low(context.reshape(length, HEADS * HEAD_DIM)))
    hidden = low_back(product(second_in, w_in) + b_in)
    active = low(jax.nn.gelu(hidden, approximate=False))
    return inputs + product(context, w_dense) + b_dense + product(active, w_out) + b_out

def reference(tokens, segments, positions, w_qkv, b_qkv, w_dense, b_dense, w_in, b_in, w_out, b_out, gain_one, shift_one, gain_two, shift_two, cotangent):
    weights = tuple((entry.astype(jnp.float32) for entry in (w_qkv, b_qkv, w_dense, b_dense, w_in, b_in, w_out, b_out, gain_one, shift_one, gain_two, shift_two)))
    pack_count = tokens.shape[0] // SEQ_LEN
    inputs = tokens.astype(jnp.float32).reshape(pack_count, SEQ_LEN, D)
    segment_rows = segments.reshape(pack_count, SEQ_LEN)
    position_rows = positions.reshape(pack_count, SEQ_LEN)
    layer = jax.checkpoint(pack_layer)

    def forward(params, data):

        def visit(running, element):
            return (running, layer(params, element[0], element[1], element[2]))
        running, results = lax.scan(visit, jnp.zeros((), jnp.float32), (data, segment_rows, position_rows))
        return results
    mixed, pullback = jax.vjp(forward, weights, inputs)
    grads, d_tokens = pullback(cotangent.astype(jnp.float32).reshape(pack_count, SEQ_LEN, D))
    return (mixed.reshape(-1, D), d_tokens.reshape(-1, D), grads[0], grads[1], grads[2], grads[3], grads[4], grads[5], grads[6], grads[7], grads[8], grads[9], grads[10], grads[11])
```

```python
import functools

import jax
import jax.numpy as jnp
from jax import lax
from jax.experimental import pallas as pl
from jax.experimental.pallas import tpu as pltpu
from jax.sharding import PartitionSpec as P

HEAD_DIM = 64
ROT = 16


norm_epsilon = 1e-05
masked_fill = -1e30


def rotary_tables(position):
    steps = jnp.arange(ROT // 2, dtype=jnp.int32).astype(jnp.float32)
    inverse = 10000.0 ** (-2.0 * steps / ROT)
    angle = position.astype(jnp.float32)[:, None] * inverse[None, :]
    angle = jnp.concatenate([angle, angle], axis=1)
    return (jnp.cos(angle), jnp.sin(angle))


def rotary(part, cosines, sines):
    turned = part[..., :ROT]
    swapped = jnp.concatenate([-turned[..., ROT // 2 :], turned[..., : ROT // 2]], axis=-1)
    rotated = turned * cosines[:, None, :] + swapped * sines[:, None, :]
    return jnp.concatenate([rotated, part[..., ROT:]], axis=-1)


def rotary_back(grads, cosines, sines):
    turned = grads[..., :ROT]
    scaled = turned * sines[:, None, :]
    swapped = jnp.concatenate([scaled[..., ROT // 2 :], -scaled[..., : ROT // 2]], axis=-1)
    return jnp.concatenate([turned * cosines[:, None, :] + swapped, grads[..., ROT:]], axis=-1)


def gelu_exact(values):
    return jax.nn.gelu(values, approximate=False)


BLOCK = 256
SWAP = [(0, 1), (1, 0)]


def attention_kernel(
    block, low_ref, seg_col, seg_row, q_ref, k_ref, v_ref, do_ref, ctx_ref, dq_ref, dk_ref, dv_ref
):
    heads, length, depth = q_ref.shape
    nt = (((1,), (1,)), ((), ()))
    tn = (((0,), (0,)), ((), ()))
    dk_ref[...] = jnp.zeros_like(dk_ref)
    dv_ref[...] = jnp.zeros_like(dv_ref)

    def query_step(i, carry):
        rows = pl.ds(pl.multiple_of(i * block, block), block)
        low = low_ref[i]
        segs = seg_col[rows, :]
        places = i * block + lax.broadcasted_iota(jnp.int32, (block, block), 0)
        queries = [q_ref[h, rows, :] for h in range(heads)]
        grads = [do_ref[h, rows, :] for h in range(heads)]

        def masked_scores(j, cols):
            key_places = j * block + lax.broadcasted_iota(jnp.int32, (block, block), 1)
            allowed = (segs == seg_row[j]) & (places >= key_places)
            return [
                jnp.where(
                    allowed,
                    lax.dot_general(
                        queries[h], k_ref[h, cols, :], nt, preferred_element_type=jnp.float32
                    ),
                    masked_fill,
                )
                for h in range(heads)
            ]

        def forward(j, state):
            cols = pl.ds(pl.multiple_of(j * block, block), block)
            scores = masked_scores(j, cols)
            out = []
            for h in range(heads):
                highest, total, acc = state[h]
                new = jnp.maximum(highest, jnp.max(scores[h], axis=1, keepdims=True))
                lifted = jnp.exp(scores[h] - new)
                shrink = jnp.exp(highest - new)
                total = total * shrink + jnp.sum(lifted, axis=1, keepdims=True)
                acc = acc * shrink + jnp.dot(
                    lifted.astype(jnp.bfloat16), v_ref[h, cols, :],
                    preferred_element_type=jnp.float32,
                )
                out.append((new, total, acc))
            return tuple(out)

        state = lax.fori_loop(
            low,
            i + 1,
            forward,
            tuple(
                (
                    jnp.full((block, 1), masked_fill, jnp.float32),
                    jnp.zeros((block, 1), jnp.float32),
                    jnp.zeros((block, depth), jnp.float32),
                )
                for _ in range(heads)
            ),
        )
        lse, inner = [], []
        for h in range(heads):
            highest, total, acc = state[h]
            context = acc / total
            ctx_ref[h, rows, :] = context.astype(jnp.bfloat16)
            lse.append(highest + jnp.log(total))
            inner.append(
                jnp.sum(context * grads[h].astype(jnp.float32), axis=1, keepdims=True)
            )

        def backward(j, state):
            cols = pl.ds(pl.multiple_of(j * block, block), block)
            scores = masked_scores(j, cols)
            out = []
            for h in range(heads):
                soft = jnp.exp(scores[h] - lse[h])
                grad_soft = lax.dot_general(
                    grads[h], v_ref[h, cols, :], nt, preferred_element_type=jnp.float32
                )
                grad_raw = (soft * (grad_soft - inner[h])).astype(jnp.bfloat16)
                out.append(
                    state[h]
                    + jnp.dot(grad_raw, k_ref[h, cols, :], preferred_element_type=jnp.float32)
                )
                dk_ref[h, cols, :] += lax.dot_general(
                    grad_raw, queries[h], tn, preferred_element_type=jnp.float32
                )
                dv_ref[h, cols, :] += lax.dot_general(
                    soft.astype(jnp.bfloat16), grads[h], tn, preferred_element_type=jnp.float32
                )
            return tuple(out)

        state = lax.fori_loop(
            low,
            i + 1,
            backward,
            tuple(jnp.zeros((block, depth), jnp.float32) for _ in range(heads)),
        )
        for h in range(heads):
            dq_ref[h, rows, :] = state[h] * HEAD_DIM ** (-0.5)
        return carry

    lax.fori_loop(0, length // block, query_step, 0)


def attention(queries, keys, values, grads, segments):
    heads, length, depth = queries.shape
    block = min(BLOCK, length)
    count = length // block
    firsts = segments.reshape(count, block)[:, 0]
    low = jnp.sum((segments[None, :] < firsts[:, None]).astype(jnp.int32), axis=1) // block
    vmem = pl.BlockSpec(memory_space=pltpu.VMEM)
    wide = jax.ShapeDtypeStruct((heads, length, depth), jnp.float32)
    return pl.pallas_call(
        functools.partial(attention_kernel, block),
        out_shape=(jax.ShapeDtypeStruct((heads, length, depth), jnp.bfloat16), wide, wide, wide),
        in_specs=[pl.BlockSpec(memory_space=pltpu.SMEM)] + [vmem] * 6,
        out_specs=(vmem,) * 4,
        compiler_params=pltpu.CompilerParams(vmem_limit_bytes=48 * 1024 * 1024),
        cost_estimate=pl.CostEstimate(
            flops=7 * 2 * heads * length * length // 4 * depth,
            bytes_accessed=heads * length * depth * 22,
            transcendentals=heads * length * length // 2,
        ),
    )(
        low,
        segments[:, None],
        segments.reshape(count, 1, block),
        queries,
        keys,
        values,
        grads,
    )


def in_order(index, mine, other, axis=0):
    return jnp.where(
        index == 0,
        jnp.concatenate([mine, other], axis=axis),
        jnp.concatenate([other, mine], axis=axis),
    )


def body(
    tokens,
    segments,
    positions,
    w_qkv,
    b_qkv,
    w_dense,
    b_dense,
    w_in,
    b_in,
    w_out,
    b_out,
    gain_one,
    shift_one,
    gain_two,
    shift_two,
    cotangent,
):
    rows_here, width = tokens.shape
    features = 2 * width
    length = segments.shape[0]
    row, col = lax.axis_index("row"), lax.axis_index("col")
    f32, bf16 = jnp.float32, jnp.bfloat16

    def swap_col(part):
        return lax.ppermute(part, "col", SWAP)

    def swap_row(part):
        return lax.ppermute(part, "row", SWAP)

    def split_half(array, axis):
        half = array.shape[axis] // 2
        mine = lax.dynamic_slice_in_dim(array, col * half, half, axis)
        other = lax.dynamic_slice_in_dim(array, (1 - col) * half, half, axis)
        return mine, other

    def whole_rows(part):
        wide = jnp.concatenate([part, swap_col(part)], axis=1)
        return in_order(row, wide, swap_row(wide))

    x_all = whole_rows(tokens)
    norms = jnp.stack([gain_one, shift_one, gain_two, shift_two])
    norms = jnp.concatenate([norms, swap_col(norms)], axis=1)

    qkv_mine, qkv_other = split_half(w_qkv, 1)
    qkv_w = jnp.concatenate([qkv_mine, swap_col(qkv_other)], axis=0)
    g_all = whole_rows(cotangent)
    dense_mine, dense_other = split_half(w_dense, 0)
    dense_w = jnp.concatenate([dense_mine, swap_col(dense_other)], axis=1)
    in_mine, in_other = split_half(w_in, 1)
    in_w = jnp.concatenate([in_mine, swap_col(in_other)], axis=0)
    out_mine, out_other = split_half(w_out, 0)
    out_w = jnp.concatenate([out_mine, swap_col(out_other)], axis=1)

    inputs = x_all.astype(f32)
    average = jnp.mean(inputs, axis=1, keepdims=True)
    spread = jnp.mean(inputs * inputs, axis=1, keepdims=True) - average * average
    inv_std = lax.rsqrt(spread + norm_epsilon)
    normed = (inputs - average) * inv_std
    first_in = (normed * norms[0] + norms[1]).astype(bf16)
    second_in = (normed * norms[2] + norms[3]).astype(bf16)

    joined = jnp.dot(first_in, qkv_w, preferred_element_type=f32) + split_half(b_qkv, 0)[0]
    joined = joined.reshape(length, -1, 3, HEAD_DIM)
    cosines, sines = rotary_tables(positions)
    query_heads = jnp.transpose(
        (rotary(joined[:, :, 0], cosines, sines)).astype(bf16) * bf16(HEAD_DIM ** (-0.5)),
        (1, 0, 2),
    )
    key_heads = jnp.transpose(rotary(joined[:, :, 1], cosines, sines).astype(bf16), (1, 0, 2))
    value_heads = jnp.transpose(joined[:, :, 2].astype(bf16), (1, 0, 2))
    d_context = jnp.dot(g_all, dense_w.T, preferred_element_type=f32).astype(bf16)
    grad_heads = jnp.transpose(d_context.reshape(length, -1, HEAD_DIM), (1, 0, 2))
    contexts, query_grads, key_grads, value_grads = attention(
        query_heads, key_heads, value_heads, grad_heads, segments
    )
    context = jnp.transpose(contexts, (1, 0, 2)).reshape(length, -1)

    hidden = jnp.dot(second_in, in_w, preferred_element_type=f32) + split_half(b_in, 0)[0]
    active = gelu_exact(hidden).astype(bf16)
    d_active = jnp.dot(g_all, out_w.T, preferred_element_type=f32)
    d_hidden = jax.vjp(gelu_exact, hidden)[1](d_active)[0].astype(bf16)

    def tn_dot(left, right):
        return lax.dot_general(left, right, (((0,), (0,)), ((), ())), preferred_element_type=f32)

    def own_rows(partial):
        mine = lax.dynamic_slice_in_dim(partial, row * rows_here, rows_here, 0)
        other = lax.dynamic_slice_in_dim(partial, (1 - row) * rows_here, rows_here, 0)
        return mine + swap_row(other.astype(bf16)).astype(f32)

    def own_block(summed):
        return summed[:, :width] + swap_col(summed[:, width:].astype(bf16)).astype(f32)

    def pack_sum(mine, other, axis):
        both = in_order(col, mine.astype(bf16), swap_col(other.astype(bf16)), axis)
        return lax.psum(both, "dp").astype(f32)

    d_out = tn_dot(active, g_all)
    d_out = pack_sum(d_out[:, :width], d_out[:, width:], 0)
    d_in = tn_dot(second_in, d_hidden)
    d_in = pack_sum(d_in[:width], d_in[width:], 1)
    d_dense = tn_dot(context, g_all)
    d_dense = pack_sum(d_dense[:, :width], d_dense[:, width:], 0)

    query_back = rotary_back(jnp.transpose(query_grads, (1, 0, 2)), cosines, sines)
    key_back = rotary_back(jnp.transpose(key_grads, (1, 0, 2)), cosines, sines)
    value_back = jnp.transpose(value_grads, (1, 0, 2))
    d_joined = (
        jnp.stack([query_back, key_back, value_back], axis=2).reshape(length, -1).astype(bf16)
    )
    d_qkv = tn_dot(first_in, d_joined)
    d_qkv = pack_sum(d_qkv[:width], d_qkv[width:], 1)

    branches = own_block(
        own_rows(
            jnp.dot(context, dense_w, preferred_element_type=f32)
            + jnp.dot(active, out_w, preferred_element_type=f32)
        )
    )
    mixed = tokens.astype(f32) + branches + b_dense + b_out

    d_first = lax.dot_general(d_joined, qkv_w, (((1,), (1,)), ((), ())), preferred_element_type=f32)
    d_second = lax.dot_general(d_hidden, in_w, (((1,), (1,)), ((), ())), preferred_element_type=f32)
    hat = own_rows(d_first * norms[0] + d_second * norms[2])
    own_inputs = lax.dynamic_slice_in_dim(x_all, row * rows_here, rows_here, 0).astype(f32)
    own_average = lax.dynamic_slice_in_dim(average, row * rows_here, rows_here, 0)
    own_std = lax.dynamic_slice_in_dim(inv_std, row * rows_here, rows_here, 0)
    own_normed = (own_inputs - own_average) * own_std
    hat_sums = jnp.stack([jnp.sum(hat, axis=1), jnp.sum(hat * own_normed, axis=1)])
    hat_means = (hat_sums + swap_col(hat_sums)) / features
    d_tokens = cotangent.astype(f32) + own_std * (
        own_block(hat)
        - hat_means[0][:, None]
        - own_normed[:, :width] * hat_means[1][:, None]
    )

    vectors = jnp.stack(
        [
            jnp.sum(d_first * normed, axis=0),
            jnp.sum(d_first, axis=0),
            jnp.sum(d_second * normed, axis=0),
            jnp.sum(d_second, axis=0),
        ]
    )
    vectors = vectors[:, :width] + swap_col(vectors[:, width:])
    vectors = jnp.concatenate([vectors, jnp.sum(cotangent, axis=0, dtype=f32)[None]], axis=0)
    vectors = vectors + swap_row(vectors)
    biases = jnp.concatenate(
        [jnp.sum(d_joined, axis=0, dtype=f32), jnp.sum(d_hidden, axis=0, dtype=f32)]
    )
    other_biases = swap_col(biases)
    small = lax.psum(jnp.concatenate([vectors.reshape(-1), biases, other_biases]), "dp")
    vectors = small[: 5 * width].reshape(5, width)
    total = biases.shape[0]
    own_bias = small[5 * width : 5 * width + total]
    other_bias = small[5 * width + total :]
    cut = d_joined.shape[1]
    d_qkv_bias = in_order(col, own_bias[:cut], other_bias[:cut])
    d_in_bias = in_order(col, own_bias[cut:], other_bias[cut:])
    return (
        mixed,
        d_tokens,
        d_qkv,
        d_qkv_bias,
        d_dense,
        vectors[4],
        d_in,
        d_in_bias,
        d_out,
        vectors[4],
        vectors[0],
        vectors[1],
        vectors[2],
        vectors[3],
    )


def solution(mesh):
    in_specs = (
        P(("dp", "row"), "col"),
        P("dp"),
        P("dp"),
        P("col", "row"),
        P("row"),
        P("row", "col"),
        P("col"),
        P("col", "row"),
        P("row"),
        P("row", "col"),
        P("col"),
        P("col"),
        P("col"),
        P("col"),
        P("col"),
        P(("dp", "row"), "col"),
    )
    out_specs = (
        P(("dp", "row"), "col"),
        P(("dp", "row"), "col"),
        P("col", "row"),
        P("row"),
        P("row", "col"),
        P("col"),
        P("col", "row"),
        P("row"),
        P("row", "col"),
        P("col"),
        P("col"),
        P("col"),
        P("col"),
        P("col"),
    )
    return jax.shard_map(body, mesh=mesh, in_specs=in_specs, out_specs=out_specs, check_vma=False)
```

```python
import functools

import jax
import jax.numpy as jnp
from jax import lax
from jax.experimental import pallas as pl
from jax.experimental.pallas import tpu as pltpu
from jax.sharding import PartitionSpec as P

HEAD_DIM = 64
ROT = 16
LANES = 128


norm_epsilon = 1e-05
masked_fill = -1e30


def lane_tables(position):
    lane = jnp.arange(LANES, dtype=jnp.int32)
    steps = (lane % (ROT // 2)).astype(jnp.float32)
    inverse = 10000.0 ** (-2.0 * steps / ROT)
    angle = position.astype(jnp.float32)[:, None] * inverse[None, :]
    sines = jnp.sin(angle)
    return (
        jnp.where(lane < ROT, jnp.cos(angle), 1.0),
        jnp.where(lane < ROT // 2, -sines, 0.0),
        jnp.where((lane >= ROT // 2) & (lane < ROT), sines, 0.0),
    )


def gelu_exact(values):
    return jax.nn.gelu(values, approximate=False)


BLOCK = 256
SWAP = [(0, 1), (1, 0)]


def attention_kernel(
    block, low_ref, seg_col, seg_row, joined_ref, do_ref, cos_ref, up_ref, down_ref,
    ctx_ref, dj_ref, q_ref, k_ref, v_ref, dk_ref, dv_ref,
):
    heads, length, depth = q_ref.shape
    nt = (((1,), (1,)), ((), ()))
    tn = (((0,), (0,)), ((), ()))

    def place(h, part):
        return slice((3 * h + part) * depth, (3 * h + part + 1) * depth)

    def turn(u, rows, sign):
        up = pltpu.roll(u, depth - ROT // 2, 1) * up_ref[rows, :]
        down = pltpu.roll(u, ROT // 2, 1) * down_ref[rows, :]
        return u * cos_ref[rows, :] + sign * (up + down)

    def query_step(i, carry):
        rows = pl.ds(pl.multiple_of(i * block, block), block)
        low = low_ref[i]
        segs = seg_col[rows, :]
        places = i * block + lax.broadcasted_iota(jnp.int32, (block, block), 0)
        for h in range(heads):
            q_ref[h, rows, :] = turn(joined_ref[rows, place(h, 0)], rows, 1.0).astype(
                jnp.bfloat16
            ) * jnp.bfloat16(HEAD_DIM ** (-0.5))
            k_ref[h, rows, :] = turn(joined_ref[rows, place(h, 1)], rows, 1.0).astype(jnp.bfloat16)
            v_ref[h, rows, :] = joined_ref[rows, place(h, 2)].astype(jnp.bfloat16)
            dk_ref[h, rows, :] = jnp.zeros((block, depth), jnp.float32)
            dv_ref[h, rows, :] = jnp.zeros((block, depth), jnp.float32)
        queries = [q_ref[h, rows, :] for h in range(heads)]
        grads = [do_ref[rows, h * depth : (h + 1) * depth] for h in range(heads)]

        def masked_scores(j, cols):
            key_places = j * block + lax.broadcasted_iota(jnp.int32, (block, block), 1)
            allowed = (segs == seg_row[j]) & (places >= key_places)
            return [
                jnp.where(
                    allowed,
                    lax.dot_general(
                        queries[h], k_ref[h, cols, :], nt, preferred_element_type=jnp.float32
                    ),
                    masked_fill,
                )
                for h in range(heads)
            ]

        def forward(j, state):
            cols = pl.ds(pl.multiple_of(j * block, block), block)
            scores = masked_scores(j, cols)
            out = []
            for h in range(heads):
                highest, total, acc = state[h]
                new = jnp.maximum(highest, jnp.max(scores[h], axis=1, keepdims=True))
                lifted = jnp.exp(scores[h] - new)
                shrink = jnp.exp(highest - new)
                total = total * shrink + jnp.sum(lifted, axis=1, keepdims=True)
                acc = acc * shrink + jnp.dot(
                    lifted.astype(jnp.bfloat16), v_ref[h, cols, :],
                    preferred_element_type=jnp.float32,
                )
                out.append((new, total, acc))
            return tuple(out)

        state = lax.fori_loop(
            low,
            i + 1,
            forward,
            tuple(
                (
                    jnp.full((block, 1), masked_fill, jnp.float32),
                    jnp.zeros((block, 1), jnp.float32),
                    jnp.zeros((block, depth), jnp.float32),
                )
                for _ in range(heads)
            ),
        )
        lse, inner = [], []
        for h in range(heads):
            highest, total, acc = state[h]
            context = acc / total
            ctx_ref[rows, h * depth : (h + 1) * depth] = context.astype(jnp.bfloat16)
            lse.append(highest + jnp.log(total))
            inner.append(
                jnp.sum(context * grads[h].astype(jnp.float32), axis=1, keepdims=True)
            )

        def backward(j, state):
            cols = pl.ds(pl.multiple_of(j * block, block), block)
            scores = masked_scores(j, cols)
            out = []
            for h in range(heads):
                soft = jnp.exp(scores[h] - lse[h])
                grad_soft = lax.dot_general(
                    grads[h], v_ref[h, cols, :], nt, preferred_element_type=jnp.float32
                )
                grad_raw = (soft * (grad_soft - inner[h])).astype(jnp.bfloat16)
                out.append(
                    state[h]
                    + jnp.dot(grad_raw, k_ref[h, cols, :], preferred_element_type=jnp.float32)
                )
                dk_ref[h, cols, :] += lax.dot_general(
                    grad_raw, queries[h], tn, preferred_element_type=jnp.float32
                )
                dv_ref[h, cols, :] += lax.dot_general(
                    soft.astype(jnp.bfloat16), grads[h], tn, preferred_element_type=jnp.float32
                )
            return tuple(out)

        state = lax.fori_loop(
            low,
            i + 1,
            backward,
            tuple(jnp.zeros((block, depth), jnp.float32) for _ in range(heads)),
        )
        for h in range(heads):
            dj_ref[rows, place(h, 0)] = turn(
                state[h] * HEAD_DIM ** (-0.5), rows, -1.0
            ).astype(jnp.bfloat16)
        return carry

    lax.fori_loop(0, length // block, query_step, 0)

    def key_step(j, carry):
        rows = pl.ds(pl.multiple_of(j * block, block), block)
        for h in range(heads):
            dj_ref[rows, place(h, 1)] = turn(dk_ref[h, rows, :], rows, -1.0).astype(jnp.bfloat16)
            dj_ref[rows, place(h, 2)] = dv_ref[h, rows, :].astype(jnp.bfloat16)
        return carry

    lax.fori_loop(0, length // block, key_step, 0)


def attention(joined, grads, tables, segments):
    length = joined.shape[0]
    heads = grads.shape[1] // LANES
    block = min(BLOCK, length)
    count = length // block
    firsts = segments.reshape(count, block)[:, 0]
    low = jnp.sum((segments[None, :] < firsts[:, None]).astype(jnp.int32), axis=1) // block
    vmem = pl.BlockSpec(memory_space=pltpu.VMEM)
    held = (heads, length, LANES)
    return pl.pallas_call(
        functools.partial(attention_kernel, block),
        out_shape=(
            jax.ShapeDtypeStruct((length, heads * LANES), jnp.bfloat16),
            jax.ShapeDtypeStruct((length, 3 * heads * LANES), jnp.bfloat16),
        ),
        in_specs=[pl.BlockSpec(memory_space=pltpu.SMEM)] + [vmem] * 7,
        out_specs=(vmem,) * 2,
        scratch_shapes=[pltpu.VMEM(held, jnp.bfloat16)] * 3 + [pltpu.VMEM(held, jnp.float32)] * 2,
        compiler_params=pltpu.CompilerParams(vmem_limit_bytes=48 * 1024 * 1024),
        cost_estimate=pl.CostEstimate(
            flops=7 * 2 * heads * length * length // 4 * LANES,
            bytes_accessed=joined.size * 8,
            transcendentals=heads * length * length // 2,
        ),
    )(
        low,
        segments[:, None],
        segments.reshape(count, 1, block),
        joined,
        grads,
        *tables,
    )


def pack_total(part):
    size = lax.axis_size("dp")
    if size & (size - 1):
        return lax.psum(part, "dp")
    step = 1
    while step < size:
        part = part + lax.ppermute(part, "dp", [(i, i ^ step) for i in range(size)])
        step *= 2
    return part


def in_order(index, mine, other, axis=0):
    return jnp.where(
        index == 0,
        jnp.concatenate([mine, other], axis=axis),
        jnp.concatenate([other, mine], axis=axis),
    )


def body(
    tokens,
    segments,
    positions,
    w_qkv,
    b_qkv,
    w_dense,
    b_dense,
    w_in,
    b_in,
    w_out,
    b_out,
    gain_one,
    shift_one,
    gain_two,
    shift_two,
    cotangent,
):
    rows_here, width = tokens.shape
    features = 2 * width
    length = segments.shape[0]
    row, col = lax.axis_index("row"), lax.axis_index("col")
    f32, bf16 = jnp.float32, jnp.bfloat16

    def swap_col(part):
        return lax.ppermute(part, "col", SWAP)

    def swap_row(part):
        return lax.ppermute(part, "row", SWAP)

    def split_half(array, axis):
        half = array.shape[axis] // 2
        mine = lax.dynamic_slice_in_dim(array, col * half, half, axis)
        other = lax.dynamic_slice_in_dim(array, (1 - col) * half, half, axis)
        return mine, other

    def whole_rows(part, part_other):
        wide = jnp.concatenate([part, part_other], axis=1)
        return in_order(row, wide, swap_row(wide))

    def tn_dot(left, right):
        return lax.dot_general(left, right, (((0,), (0,)), ((), ())), preferred_element_type=f32)

    def nt_dot(left, right):
        return lax.dot_general(left, right, (((1,), (1,)), ((), ())), preferred_element_type=f32)

    hold = lax.optimization_barrier
    norms = jnp.stack([gain_one, shift_one, gain_two, shift_two])
    norms_other = swap_col(norms)
    norms = jnp.concatenate([norms, norms_other], axis=1)
    tokens_other = swap_col(tokens)
    in_mine, in_other = split_half(w_in, 1)
    out_mine, out_other = split_half(w_out, 0)
    qkv_mine, qkv_other = split_half(w_qkv, 1)
    dense_mine, dense_other = split_half(w_dense, 0)
    tokens_other, in_other, cotangent_late = hold((tokens_other, in_other, cotangent))
    x_all = whole_rows(tokens, tokens_other)
    in_other = swap_col(in_other)
    cotangent_other = swap_col(cotangent_late)
    in_other, out_other, qkv_other, dense_other = hold(
        (in_other, out_other, qkv_other, dense_other)
    )
    in_w = jnp.concatenate([in_mine, in_other], axis=0)
    out_w = jnp.concatenate([out_mine, swap_col(out_other)], axis=1)
    g_all = whole_rows(cotangent, cotangent_other)
    qkv_w = jnp.concatenate([qkv_mine, swap_col(qkv_other)], axis=0)
    dense_w = jnp.concatenate([dense_mine, swap_col(dense_other)], axis=1)

    qkv_half = qkv_w.shape[1]
    heads = qkv_half // (3 * HEAD_DIM)
    parts = 3 * heads
    narrow = jnp.arange(qkv_half, dtype=jnp.int32)
    spread_out = (
        (narrow // HEAD_DIM * LANES + narrow % HEAD_DIM)[:, None]
        == jnp.arange(parts * LANES, dtype=jnp.int32)[None, :]
    ).astype(bf16)
    qkv_wide = jnp.dot(qkv_w, spread_out, preferred_element_type=f32).astype(bf16)
    gap = LANES - HEAD_DIM
    qkv_bias = jnp.pad(
        split_half(b_qkv, 0)[0].reshape(parts, HEAD_DIM), ((0, 0), (0, gap))
    ).reshape(-1)
    dense_wide = jnp.pad(
        dense_w.reshape(heads, HEAD_DIM, features), ((0, 0), (0, gap), (0, 0))
    ).reshape(heads * LANES, features)
    tables = lane_tables(positions)

    inputs = x_all.astype(f32)
    average = jnp.mean(inputs, axis=1, keepdims=True)
    spread = jnp.mean(inputs * inputs, axis=1, keepdims=True) - average * average
    inv_std = lax.rsqrt(spread + norm_epsilon)
    normed = (inputs - average) * inv_std
    first_in = (normed * norms[0] + norms[1]).astype(bf16)
    second_in = (normed * norms[2] + norms[3]).astype(bf16)

    hidden = jnp.dot(second_in, in_w, preferred_element_type=f32) + split_half(b_in, 0)[0]
    active = gelu_exact(hidden).astype(bf16)
    d_active = nt_dot(g_all, out_w)
    d_hidden = jax.vjp(gelu_exact, hidden)[1](d_active)[0].astype(bf16)
    d_out = tn_dot(active, g_all).astype(bf16)
    d_in = tn_dot(second_in, d_hidden).astype(bf16)

    first_in, d_out, d_in, g_late = hold((first_in, d_out, d_in, g_all))
    joined = jnp.dot(first_in, qkv_wide, preferred_element_type=f32) + qkv_bias
    d_context = nt_dot(g_late, dense_wide).astype(bf16)
    context, d_joined = attention(joined, d_context, tables, segments)

    def own_rows(partial):
        mine = lax.dynamic_slice_in_dim(partial, row * rows_here, rows_here, 0)
        other = lax.dynamic_slice_in_dim(partial, (1 - row) * rows_here, rows_here, 0)
        return mine + swap_row(other.astype(bf16)).astype(f32)

    def own_block(summed):
        return summed[:, :width] + swap_col(summed[:, width:].astype(bf16)).astype(f32)

    def pair(mine, other, axis):
        return in_order(col, mine, swap_col(other), axis)

    d_out, d_in = lax.psum(
        (pair(d_out[:, :width], d_out[:, width:], 0), pair(d_in[:width], d_in[width:], 1)), "dp"
    )
    d_dense = tn_dot(context, g_all).astype(bf16)
    d_dense = d_dense.reshape(heads, LANES, features)[:, :HEAD_DIM].reshape(-1, features)
    d_qkv = nt_dot(tn_dot(first_in, d_joined).astype(bf16), spread_out).astype(bf16)
    d_dense = pair(d_dense[:, :width], d_dense[:, width:], 0)
    d_qkv = pair(d_qkv[:width], d_qkv[width:], 1)
    d_out, d_in, d_dense, d_qkv = hold((d_out, d_in, d_dense, d_qkv))
    d_dense, d_qkv = lax.psum((d_dense, d_qkv), "dp")
    d_out, d_in, d_dense, d_qkv = (part.astype(f32) for part in (d_out, d_in, d_dense, d_qkv))

    branches = own_block(
        own_rows(
            jnp.dot(context, dense_wide, preferred_element_type=f32)
            + jnp.dot(active, out_w, preferred_element_type=f32)
        )
    )
    mixed = tokens.astype(f32) + branches + b_dense + b_out

    d_first = nt_dot(d_joined, qkv_wide)
    d_second = nt_dot(d_hidden, in_w)
    hat = own_rows(d_first * norms[0] + d_second * norms[2])
    own_inputs = lax.dynamic_slice_in_dim(x_all, row * rows_here, rows_here, 0).astype(f32)
    own_average = lax.dynamic_slice_in_dim(average, row * rows_here, rows_here, 0)
    own_std = lax.dynamic_slice_in_dim(inv_std, row * rows_here, rows_here, 0)
    own_normed = (own_inputs - own_average) * own_std
    hat_sums = jnp.stack([jnp.sum(hat, axis=1), jnp.sum(hat * own_normed, axis=1)])
    hat_means = (hat_sums + swap_col(hat_sums)) / features
    d_tokens = cotangent.astype(f32) + own_std * (
        own_block(hat)
        - hat_means[0][:, None]
        - own_normed[:, :width] * hat_means[1][:, None]
    )

    vectors = jnp.stack(
        [
            jnp.sum(d_first * normed, axis=0),
            jnp.sum(d_first, axis=0),
            jnp.sum(d_second * normed, axis=0),
            jnp.sum(d_second, axis=0),
        ]
    )
    vectors = vectors[:, :width] + swap_col(vectors[:, width:])
    vectors = jnp.concatenate([vectors, jnp.sum(cotangent, axis=0, dtype=f32)[None]], axis=0)
    vectors = vectors + swap_row(vectors)
    biases = jnp.concatenate(
        [
            jnp.sum(d_joined, axis=0, dtype=f32).reshape(parts, LANES)[:, :HEAD_DIM].reshape(-1),
            jnp.sum(d_hidden, axis=0, dtype=f32),
        ]
    )
    other_biases = swap_col(biases)
    small = pack_total(jnp.concatenate([vectors.reshape(-1), biases, other_biases]))
    vectors = small[: 5 * width].reshape(5, width)
    total = biases.shape[0]
    own_bias = small[5 * width : 5 * width + total]
    other_bias = small[5 * width + total :]
    cut = qkv_half
    d_qkv_bias = in_order(col, own_bias[:cut], other_bias[:cut])
    d_in_bias = in_order(col, own_bias[cut:], other_bias[cut:])
    return (
        mixed,
        d_tokens,
        d_qkv,
        d_qkv_bias,
        d_dense,
        vectors[4],
        d_in,
        d_in_bias,
        d_out,
        vectors[4],
        vectors[0],
        vectors[1],
        vectors[2],
        vectors[3],
    )


def solution(mesh):
    in_specs = (
        P(("dp", "row"), "col"),
        P("dp"),
        P("dp"),
        P("col", "row"),
        P("row"),
        P("row", "col"),
        P("col"),
        P("col", "row"),
        P("row"),
        P("row", "col"),
        P("col"),
        P("col"),
        P("col"),
        P("col"),
        P("col"),
        P(("dp", "row"), "col"),
    )
    out_specs = (
        P(("dp", "row"), "col"),
        P(("dp", "row"), "col"),
        P("col", "row"),
        P("row"),
        P("row", "col"),
        P("col"),
        P("col", "row"),
        P("row"),
        P("row", "col"),
        P("col"),
        P("col"),
        P("col"),
        P("col"),
        P("col"),
    )
    return jax.shard_map(body, mesh=mesh, in_specs=in_specs, out_specs=out_specs, check_vma=False)
```

```python
import functools

import jax
import jax.numpy as jnp
from jax import lax
from jax.experimental import pallas as pl
from jax.experimental.pallas import tpu as pltpu
from jax.sharding import PartitionSpec as P

HEAD_DIM = 64
ROT = 16
LANES = 128


norm_epsilon = 1e-05
masked_fill = -1e30


def lane_tables(position):
    lane = jnp.arange(LANES, dtype=jnp.int32)
    steps = (lane % (ROT // 2)).astype(jnp.float32)
    inverse = 10000.0 ** (-2.0 * steps / ROT)
    angle = position.astype(jnp.float32)[:, None] * inverse[None, :]
    sines = jnp.sin(angle)
    return (
        jnp.where(lane < ROT, jnp.cos(angle), 1.0),
        jnp.where(lane < ROT // 2, -sines, 0.0),
        jnp.where((lane >= ROT // 2) & (lane < ROT), sines, 0.0),
    )


def gelu_exact(values):
    return jax.nn.gelu(values, approximate=False)


BLOCK = 256
SWAP = [(0, 1), (1, 0)]


def attention_kernel(
    block, low_ref, seg_col, seg_row, joined_ref, do_ref, cos_ref, up_ref, down_ref,
    ctx_ref, dj_ref, q_ref, k_ref, v_ref, dk_ref, dv_ref,
):
    heads, length, depth = q_ref.shape
    nt = (((1,), (1,)), ((), ()))
    tn = (((0,), (0,)), ((), ()))

    def place(h, part):
        return slice((3 * h + part) * depth, (3 * h + part + 1) * depth)

    def turn(u, rows, sign):
        up = pltpu.roll(u, depth - ROT // 2, 1) * up_ref[rows, :]
        down = pltpu.roll(u, ROT // 2, 1) * down_ref[rows, :]
        return u * cos_ref[rows, :] + sign * (up + down)

    def query_step(i, carry):
        rows = pl.ds(pl.multiple_of(i * block, block), block)
        low = low_ref[i]
        segs = seg_col[rows, :]
        places = i * block + lax.broadcasted_iota(jnp.int32, (block, block), 0)
        for h in range(heads):
            q_ref[h, rows, :] = turn(joined_ref[rows, place(h, 0)], rows, 1.0).astype(
                jnp.bfloat16
            ) * jnp.bfloat16(HEAD_DIM ** (-0.5))
            k_ref[h, rows, :] = turn(joined_ref[rows, place(h, 1)], rows, 1.0).astype(jnp.bfloat16)
            v_ref[h, rows, :] = joined_ref[rows, place(h, 2)].astype(jnp.bfloat16)
            dk_ref[h, rows, :] = jnp.zeros((block, depth), jnp.float32)
            dv_ref[h, rows, :] = jnp.zeros((block, depth), jnp.float32)
        queries = [q_ref[h, rows, :] for h in range(heads)]
        grads = [do_ref[rows, h * depth : (h + 1) * depth] for h in range(heads)]

        def masked_scores(j, cols):
            key_places = j * block + lax.broadcasted_iota(jnp.int32, (block, block), 1)
            allowed = (segs == seg_row[j]) & (places >= key_places)
            return [
                jnp.where(
                    allowed,
                    lax.dot_general(
                        queries[h], k_ref[h, cols, :], nt, preferred_element_type=jnp.float32
                    ),
                    masked_fill,
                )
                for h in range(heads)
            ]

        def forward(j, state):
            cols = pl.ds(pl.multiple_of(j * block, block), block)
            scores = masked_scores(j, cols)
            out = []
            for h in range(heads):
                highest, total, acc = state[h]
                new = jnp.maximum(highest, jnp.max(scores[h], axis=1, keepdims=True))
                lifted = jnp.exp(scores[h] - new)
                shrink = jnp.exp(highest - new)
                total = total * shrink + jnp.sum(lifted, axis=1, keepdims=True)
                acc = acc * shrink + jnp.dot(
                    lifted.astype(jnp.bfloat16), v_ref[h, cols, :],
                    preferred_element_type=jnp.float32,
                )
                out.append((new, total, acc))
            return tuple(out)

        state = lax.fori_loop(
            low,
            i + 1,
            forward,
            tuple(
                (
                    jnp.full((block, 1), masked_fill, jnp.float32),
                    jnp.zeros((block, 1), jnp.float32),
                    jnp.zeros((block, depth), jnp.float32),
                )
                for _ in range(heads)
            ),
        )
        lse, inner = [], []
        for h in range(heads):
            highest, total, acc = state[h]
            context = acc / total
            ctx_ref[rows, h * depth : (h + 1) * depth] = context.astype(jnp.bfloat16)
            lse.append(highest + jnp.log(total))
            inner.append(
                jnp.sum(context * grads[h].astype(jnp.float32), axis=1, keepdims=True)
            )

        def backward(j, state):
            cols = pl.ds(pl.multiple_of(j * block, block), block)
            scores = masked_scores(j, cols)
            out = []
            for h in range(heads):
                soft = jnp.exp(scores[h] - lse[h])
                grad_soft = lax.dot_general(
                    grads[h], v_ref[h, cols, :], nt, preferred_element_type=jnp.float32
                )
                grad_raw = (soft * (grad_soft - inner[h])).astype(jnp.bfloat16)
                out.append(
                    state[h]
                    + jnp.dot(grad_raw, k_ref[h, cols, :], preferred_element_type=jnp.float32)
                )
                dk_ref[h, cols, :] += lax.dot_general(
                    grad_raw, queries[h], tn, preferred_element_type=jnp.float32
                )
                dv_ref[h, cols, :] += lax.dot_general(
                    soft.astype(jnp.bfloat16), grads[h], tn, preferred_element_type=jnp.float32
                )
            return tuple(out)

        state = lax.fori_loop(
            low,
            i + 1,
            backward,
            tuple(jnp.zeros((block, depth), jnp.float32) for _ in range(heads)),
        )
        for h in range(heads):
            dj_ref[rows, place(h, 0)] = turn(
                state[h] * HEAD_DIM ** (-0.5), rows, -1.0
            ).astype(jnp.bfloat16)
        return carry

    lax.fori_loop(0, length // block, query_step, 0)

    def key_step(j, carry):
        rows = pl.ds(pl.multiple_of(j * block, block), block)
        for h in range(heads):
            dj_ref[rows, place(h, 1)] = turn(dk_ref[h, rows, :], rows, -1.0).astype(jnp.bfloat16)
            dj_ref[rows, place(h, 2)] = dv_ref[h, rows, :].astype(jnp.bfloat16)
        return carry

    lax.fori_loop(0, length // block, key_step, 0)


def attention(joined, grads, tables, segments):
    length = joined.shape[0]
    heads = grads.shape[1] // LANES
    block = min(BLOCK, length)
    count = length // block
    firsts = segments.reshape(count, block)[:, 0]
    low = jnp.sum((segments[None, :] < firsts[:, None]).astype(jnp.int32), axis=1) // block
    vmem = pl.BlockSpec(memory_space=pltpu.VMEM)
    held = (heads, length, LANES)
    return pl.pallas_call(
        functools.partial(attention_kernel, block),
        out_shape=(
            jax.ShapeDtypeStruct((length, heads * LANES), jnp.bfloat16),
            jax.ShapeDtypeStruct((length, 3 * heads * LANES), jnp.bfloat16),
        ),
        in_specs=[pl.BlockSpec(memory_space=pltpu.SMEM)] + [vmem] * 7,
        out_specs=(vmem,) * 2,
        scratch_shapes=[pltpu.VMEM(held, jnp.bfloat16)] * 3 + [pltpu.VMEM(held, jnp.float32)] * 2,
        compiler_params=pltpu.CompilerParams(vmem_limit_bytes=48 * 1024 * 1024),
        cost_estimate=pl.CostEstimate(
            flops=7 * 2 * heads * length * length // 4 * LANES,
            bytes_accessed=joined.size * 8,
            transcendentals=heads * length * length // 2,
        ),
    )(
        low,
        segments[:, None],
        segments.reshape(count, 1, block),
        joined,
        grads,
        *tables,
    )


def pack_total(part):
    size = lax.axis_size("dp")
    if size & (size - 1):
        return lax.psum(part, "dp")
    step = 1
    while step < size:
        part = part + lax.ppermute(part, "dp", [(i, i ^ step) for i in range(size)])
        step *= 2
    return part


def in_order(index, mine, other, axis=0):
    return jnp.where(
        index == 0,
        jnp.concatenate([mine, other], axis=axis),
        jnp.concatenate([other, mine], axis=axis),
    )


def body(
    tokens,
    segments,
    positions,
    w_qkv,
    b_qkv,
    w_dense,
    b_dense,
    w_in,
    b_in,
    w_out,
    b_out,
    gain_one,
    shift_one,
    gain_two,
    shift_two,
    cotangent,
):
    rows_here, width = tokens.shape
    features = 2 * width
    length = segments.shape[0]
    row, col = lax.axis_index("row"), lax.axis_index("col")
    f32, bf16 = jnp.float32, jnp.bfloat16

    def swap_col(part):
        return lax.ppermute(part, "col", SWAP)

    def swap_row(part):
        return lax.ppermute(part, "row", SWAP)

    def split_half(array, axis):
        half = array.shape[axis] // 2
        mine = lax.dynamic_slice_in_dim(array, col * half, half, axis)
        other = lax.dynamic_slice_in_dim(array, (1 - col) * half, half, axis)
        return mine, other

    def whole_rows(part, part_other):
        wide = jnp.concatenate([part, part_other], axis=1)
        return in_order(row, wide, swap_row(wide))

    def tn_dot(left, right):
        return lax.dot_general(left, right, (((0,), (0,)), ((), ())), preferred_element_type=f32)

    def nt_dot(left, right):
        return lax.dot_general(left, right, (((1,), (1,)), ((), ())), preferred_element_type=f32)

    hold = lax.optimization_barrier
    norms = jnp.stack([gain_one, shift_one, gain_two, shift_two])
    norms_other = swap_col(norms)
    norms = jnp.concatenate([norms, norms_other], axis=1)
    tokens_other = swap_col(tokens)
    in_mine, in_other = split_half(w_in, 1)
    out_mine, out_other = split_half(w_out, 0)
    qkv_mine, qkv_other = split_half(w_qkv, 1)
    dense_mine, dense_other = split_half(w_dense, 0)
    tokens_other, in_other, cotangent_late = hold((tokens_other, in_other, cotangent))
    x_all = whole_rows(tokens, tokens_other)
    in_other = swap_col(in_other)
    cotangent_other = swap_col(cotangent_late)
    in_other, out_other, qkv_other, dense_other = hold(
        (in_other, out_other, qkv_other, dense_other)
    )
    in_w = jnp.concatenate([in_mine, in_other], axis=0)
    out_w = jnp.concatenate([out_mine, swap_col(out_other)], axis=1)
    g_all = whole_rows(cotangent, cotangent_other)
    qkv_w = jnp.concatenate([qkv_mine, swap_col(qkv_other)], axis=0)
    dense_w = jnp.concatenate([dense_mine, swap_col(dense_other)], axis=1)

    qkv_half = qkv_w.shape[1]
    heads = qkv_half // (3 * HEAD_DIM)
    parts = 3 * heads
    narrow = jnp.arange(qkv_half, dtype=jnp.int32)
    spread_out = (
        (narrow // HEAD_DIM * LANES + narrow % HEAD_DIM)[:, None]
        == jnp.arange(parts * LANES, dtype=jnp.int32)[None, :]
    ).astype(bf16)
    qkv_wide = jnp.dot(qkv_w, spread_out, preferred_element_type=f32).astype(bf16)
    gap = LANES - HEAD_DIM
    qkv_bias = jnp.pad(
        split_half(b_qkv, 0)[0].reshape(parts, HEAD_DIM), ((0, 0), (0, gap))
    ).reshape(-1)
    dense_wide = jnp.pad(
        dense_w.reshape(heads, HEAD_DIM, features), ((0, 0), (0, gap), (0, 0))
    ).reshape(heads * LANES, features)
    tables = lane_tables(positions)

    inputs = x_all.astype(f32)
    average = jnp.mean(inputs, axis=1, keepdims=True)
    spread = jnp.mean(inputs * inputs, axis=1, keepdims=True) - average * average
    inv_std = lax.rsqrt(spread + norm_epsilon)
    normed = (inputs - average) * inv_std
    first_in = (normed * norms[0] + norms[1]).astype(bf16)
    second_in = (normed * norms[2] + norms[3]).astype(bf16)

    hidden = jnp.dot(second_in, in_w, preferred_element_type=f32) + split_half(b_in, 0)[0]
    active = gelu_exact(hidden).astype(bf16)
    d_active = nt_dot(g_all, out_w)
    d_hidden = jax.vjp(gelu_exact, hidden)[1](d_active)[0].astype(bf16)
    d_out = tn_dot(active, g_all).astype(bf16)
    d_in = tn_dot(second_in, d_hidden).astype(bf16)

    first_in, d_out, d_in, g_late = hold((first_in, d_out, d_in, g_all))
    joined = jnp.dot(first_in, qkv_wide, preferred_element_type=f32) + qkv_bias
    d_context = nt_dot(g_late, dense_wide).astype(bf16)
    def pair(mine, other, axis):
        return in_order(col, mine, swap_col(other), axis)

    d_out = pair(d_out[:, :width], d_out[:, width:], 0)
    d_in = pair(d_in[:width], d_in[width:], 1)
    joined, d_context, d_out, d_in = hold((joined, d_context, d_out, d_in))
    d_out, d_in = lax.psum((d_out, d_in), "dp")
    context, d_joined = attention(joined, d_context, tables, segments)

    def own_rows(partial):
        mine = lax.dynamic_slice_in_dim(partial, row * rows_here, rows_here, 0)
        other = lax.dynamic_slice_in_dim(partial, (1 - row) * rows_here, rows_here, 0)
        return mine + swap_row(other.astype(bf16)).astype(f32)

    def own_block(summed):
        return summed[:, :width] + swap_col(summed[:, width:].astype(bf16)).astype(f32)

    d_dense = tn_dot(context, g_all).astype(bf16)
    d_dense = d_dense.reshape(heads, LANES, features)[:, :HEAD_DIM].reshape(-1, features)
    d_qkv = nt_dot(tn_dot(first_in, d_joined).astype(bf16), spread_out).astype(bf16)
    d_dense = pair(d_dense[:, :width], d_dense[:, width:], 0)
    d_qkv = pair(d_qkv[:width], d_qkv[width:], 1)
    d_out, d_in, d_dense, d_qkv = hold((d_out, d_in, d_dense, d_qkv))
    d_dense, d_qkv = lax.psum((d_dense, d_qkv), "dp")
    d_out, d_in, d_dense, d_qkv = (part.astype(f32) for part in (d_out, d_in, d_dense, d_qkv))

    branches = own_block(
        own_rows(
            jnp.dot(context, dense_wide, preferred_element_type=f32)
            + jnp.dot(active, out_w, preferred_element_type=f32)
        )
    )
    mixed = tokens.astype(f32) + branches + b_dense + b_out

    d_first = nt_dot(d_joined, qkv_wide)
    d_second = nt_dot(d_hidden, in_w)
    hat = own_rows(d_first * norms[0] + d_second * norms[2])
    own_inputs = lax.dynamic_slice_in_dim(x_all, row * rows_here, rows_here, 0).astype(f32)
    own_average = lax.dynamic_slice_in_dim(average, row * rows_here, rows_here, 0)
    own_std = lax.dynamic_slice_in_dim(inv_std, row * rows_here, rows_here, 0)
    own_normed = (own_inputs - own_average) * own_std
    hat_sums = jnp.stack([jnp.sum(hat, axis=1), jnp.sum(hat * own_normed, axis=1)])
    hat_means = (hat_sums + swap_col(hat_sums)) / features
    d_tokens = cotangent.astype(f32) + own_std * (
        own_block(hat)
        - hat_means[0][:, None]
        - own_normed[:, :width] * hat_means[1][:, None]
    )

    vectors = jnp.stack(
        [
            jnp.sum(d_first * normed, axis=0),
            jnp.sum(d_first, axis=0),
            jnp.sum(d_second * normed, axis=0),
            jnp.sum(d_second, axis=0),
        ]
    )
    vectors = vectors[:, :width] + swap_col(vectors[:, width:])
    vectors = jnp.concatenate([vectors, jnp.sum(cotangent, axis=0, dtype=f32)[None]], axis=0)
    vectors = vectors + swap_row(vectors)
    biases = jnp.concatenate(
        [
            jnp.sum(d_joined, axis=0, dtype=f32).reshape(parts, LANES)[:, :HEAD_DIM].reshape(-1),
            jnp.sum(d_hidden, axis=0, dtype=f32),
        ]
    )
    other_biases = swap_col(biases)
    small = pack_total(jnp.concatenate([vectors.reshape(-1), biases, other_biases]))
    vectors = small[: 5 * width].reshape(5, width)
    total = biases.shape[0]
    own_bias = small[5 * width : 5 * width + total]
    other_bias = small[5 * width + total :]
    cut = qkv_half
    d_qkv_bias = in_order(col, own_bias[:cut], other_bias[:cut])
    d_in_bias = in_order(col, own_bias[cut:], other_bias[cut:])
    return (
        mixed,
        d_tokens,
        d_qkv,
        d_qkv_bias,
        d_dense,
        vectors[4],
        d_in,
        d_in_bias,
        d_out,
        vectors[4],
        vectors[0],
        vectors[1],
        vectors[2],
        vectors[3],
    )


def solution(mesh):
    in_specs = (
        P(("dp", "row"), "col"),
        P("dp"),
        P("dp"),
        P("col", "row"),
        P("row"),
        P("row", "col"),
        P("col"),
        P("col", "row"),
        P("row"),
        P("row", "col"),
        P("col"),
        P("col"),
        P("col"),
        P("col"),
        P("col"),
        P(("dp", "row"), "col"),
    )
    out_specs = (
        P(("dp", "row"), "col"),
        P(("dp", "row"), "col"),
        P("col", "row"),
        P("row"),
        P("row", "col"),
        P("col"),
        P("col", "row"),
        P("row"),
        P("row", "col"),
        P("col"),
        P("col"),
        P("col"),
        P("col"),
        P("col"),
    )
    return jax.shard_map(body, mesh=mesh, in_specs=in_specs, out_specs=out_specs, check_vma=False)
```
